32 devices in a mesh: tile: 8 (over z, y), lev: 4 (over x, core).
Axes of the slice: x: 2, y: 2, z: 4, core: 2. Of those that a mesh axis runs over, the one named last changes fastest.
Arguments:
- state: bfloat16 [4, 64, 512, 64], P(None, 'lev', 'tile'), may hold values from -6 to 6
- state_cotangent: bfloat16 [4, 64, 512, 64], P(None, 'lev', 'tile'), may hold values from -6 to 6
- diffusion: float32 [512, 64], P('tile'), may hold values from 0.05 to 0.24
- remap_weight: float32 [64, 4], replicated, may hold values from 0.05 to 0.5
- remap_band: int32 [64], replicated, may hold values from 0 to 60, as said below
- edge_table: int32 [8, 4, 4], P('tile'), may hold values from 0 to 7, as said below
- w_in: bfloat16 [1024, 256], replicated, may hold values from -0.375 to 0.375
- w_out: bfloat16 [256, 1024], replicated, may hold values from -0.1875 to 0.1875
Outputs:
- state_out: bfloat16 [4, 64, 512, 64], P(None, 'lev', 'tile')
- grad_state: bfloat16 [4, 64, 512, 64], P(None, 'lev', 'tile')
- grad_w_in: float32 [1024, 256], replicated
- grad_w_out: float32 [256, 1024], replicated
The draws below stay inside these ranges and needn't reach their ends.
Inputs may be any that keep to these rules, and one draw needn't show every extreme that they name: `edge_table`: entry [t, e] describes edge e of tile t (0 first row, 1 last row, 2 first column, 3 last column): [t, e, 0] is the tile across it, [t, e, 1] that tile's matching edge, [t, e, 2] is 1 where the strip runs reversed and 0 else, [t, e, 3] the quarter turns 0 to 3 of the vector components. The matching is symmetric: the partner's entry points back, with the same reversal and the opposite turns modulo 4. The four edges of a tile meet four different tiles, none of them the tile itself. remap_band[k] lies between k - 2 and k + 1, clipped to the range; remap_band[0] is 0.
All inputs are finite; a program needn't handle non-finite values.
Results may differ from the reference program's by a relative error of at most 0.0075.
Values may be sent and summed in bfloat16 or wider, within the bound.
A program may use at most 128 MiB of HBM per device.

```python
import math
import jax
import jax.numpy as jnp
from jax import lax

SIDE = 64
LEVELS = 64
UNITS = 1024
BAND = 4
FEATURES = 256
TILES = 8
COLUMNS = 32768


def draw_edge_table(key, part):
    subkeys = jax.random.split(key, 5)
    labels = jax.random.permutation(subkeys[0], TILES).astype(jnp.int32)
    flip_rows = jax.random.randint(subkeys[1], (TILES,), 0, 2).astype(jnp.int32)
    flip_cols = jax.random.randint(subkeys[2], (TILES,), 0, 2).astype(jnp.int32)
    turn_rows = jax.random.randint(subkeys[3], (TILES,), 0, 4).astype(jnp.int32)
    turn_cols = jax.random.randint(subkeys[4], (TILES,), 0, 4).astype(jnp.int32)
    position = jnp.arange(TILES, dtype=jnp.int32)
    partner = jnp.stack([(position - 1) % TILES, (position + 1) % TILES, (position - 3) % TILES, (position + 3) % TILES], axis=1)
    matching = jnp.broadcast_to(jnp.array([1, 0, 3, 2], jnp.int32), (TILES, 4))
    flips = jnp.stack([jnp.roll(flip_rows, 1), flip_rows, jnp.roll(flip_cols, 3), flip_cols], axis=1)
    turns = jnp.stack([(4 - jnp.roll(turn_rows, 1)) % 4, turn_rows, (4 - jnp.roll(turn_cols, 3)) % 4, turn_cols], axis=1)
    entries = jnp.stack([labels[partner], matching, flips, turns], axis=2).astype(jnp.int32)
    return jnp.zeros((TILES, 4, 4), jnp.int32).at[labels].set(entries)


def draw_remap_band(key, part):
    level_ids = jnp.arange(LEVELS, dtype=jnp.int32)
    jitter = jax.random.randint(key, (LEVELS,), 0, 4).astype(jnp.int32)
    starts = jnp.clip(level_ids - 2 + jitter, 0, LEVELS - BAND)
    return jnp.where(level_ids == 0, 0, starts).astype(jnp.int32)


def block_scale(own_key, shape, cuts, least, high):
    def one(dim, parts):
        draws = jax.random.uniform(jax.random.fold_in(jax.random.fold_in(own_key, 6), dim), (parts,), jnp.float32, least / len(cuts), high / len(cuts))
        return jnp.repeat(jnp.exp(draws), shape[dim] // parts).reshape((-1,) + (1,) * (len(shape) - dim - 1))

    factor_of = one(*cuts[0])
    for cut in cuts[1:]:
        factor_of = factor_of * one(*cut)
    return factor_of


def centred(stream_key, shape, scale, limit, cuts=(), held_as=jnp.bfloat16):
    result = jax.random.normal(stream_key, shape, jnp.float32) * scale
    if len(cuts) > 0:
        result = block_scale(stream_key, shape, cuts, -0.22, 0.18) * result
    return jnp.clip(result, min=-limit, max=limit).astype(held_as)


def setup_inputs(seed: int = 0) -> dict:
    seeds = jax.random.split(jax.random.key(seed), 9)
    return {
        "state": centred(seeds[0], (4, LEVELS, TILES * SIDE, SIDE), 1.0, 6.0, ((1, 4), (2, 8))),
        "state_cotangent": centred(seeds[1], (4, LEVELS, TILES * SIDE, SIDE), 1.0, 6.0, ((1, 4), (2, 8))),
        "diffusion": jnp.clip(jnp.exp(math.log(0.24) - 1.5686159 * jax.random.uniform(seeds[2], (TILES * SIDE, SIDE), jnp.float32) ** block_scale(seeds[2], (TILES * SIDE, SIDE), ((0, 8),), -0.2, 0.2)), 0.05, 0.24),
        "remap_weight": jnp.clip(jax.random.uniform(seeds[3], (LEVELS, BAND), jnp.float32, 0.05, 0.5), 0.05, 0.5),
        "remap_band": draw_remap_band(jax.random.fold_in(seeds[8], 71), 0),
        "edge_table": draw_edge_table(jax.random.fold_in(seeds[8], 71), 0),
        "w_in": centred(seeds[6], (UNITS, FEATURES), FEATURES ** -0.5, 0.375),
        "w_out": centred(seeds[7], (FEATURES, UNITS), UNITS ** -0.5, 0.1875),
    }


def edge_strips(blocks):
    return jnp.stack([blocks[:, :, :, 0, :], blocks[:, :, :, -1, :], blocks[:, :, :, :, 0], blocks[:, :, :, :, -1]], axis=1)

def orient(strip, flipped, quarter):
    strip = jnp.where(flipped == 1, strip[..., ::-1], strip)
    cosine = (quarter == 0).astype(jnp.float32) - (quarter == 2).astype(jnp.float32)
    sine_part = (quarter == 1).astype(jnp.float32) - (quarter == 3).astype(jnp.float32)
    first = strip[0].astype(jnp.float32)
    second = strip[1].astype(jnp.float32)
    turned = jnp.stack([cosine * first - sine_part * second, sine_part * first + cosine * second]).astype(strip.dtype)
    return jnp.concatenate([turned, strip[2:]], axis=0)

def tile_halos(blocks, table):
    strips = edge_strips(blocks)

    def for_tile(row):

        def for_edge(entry):
            return orient(strips[entry[0], entry[1]], entry[2], entry[3])
        return jax.vmap(for_edge)(row)
    return jax.vmap(for_tile)(table)

def neighbour_sum(block, halos):
    upper = jnp.concatenate([halos[0][:, :, None, :], block[:, :, :-1, :]], axis=2)
    lower = jnp.concatenate([block[:, :, 1:, :], halos[1][:, :, None, :]], axis=2)
    before = jnp.concatenate([halos[2][:, :, :, None], block[:, :, :, :-1]], axis=3)
    after = jnp.concatenate([block[:, :, :, 1:], halos[3][:, :, :, None]], axis=3)
    return upper + lower + before + after

def remap_matrix(weight, band):
    level_ids = jnp.arange(weight.shape[0], dtype=jnp.int32)
    matrix = jnp.zeros((weight.shape[0], weight.shape[0]), weight.dtype)
    for offset in range(weight.shape[1]):
        hits = (level_ids[None, :] == (band + offset)[:, None]).astype(weight.dtype)
        matrix = matrix + weight[:, offset][:, None] * hits
    return matrix

def band_remap(columns, weight, band):
    total = jnp.zeros(columns.shape, weight.dtype)
    for offset in range(weight.shape[1]):
        picked = jnp.take(columns, (band + offset).astype(jnp.int32), axis=1).astype(weight.dtype)
        total = total + weight[:, offset][None, :, None] * picked
    return total.astype(jnp.bfloat16)

def reference(state, state_cotangent, diffusion, remap_weight, remap_band, edge_table, w_in, w_out):
    blocks = state.reshape(4, LEVELS, TILES, SIDE, SIDE).transpose(2, 0, 1, 3, 4)
    cotangents = state_cotangent.reshape(4, LEVELS, TILES, SIDE, SIDE).transpose(2, 0, 1, 3, 4)
    coeffs = diffusion.reshape(TILES, SIDE, SIDE)
    halos = tile_halos(blocks, edge_table)
    matrix = remap_matrix(remap_weight, remap_band)

    def one_tile(carry, inputs):
        grad_in, grad_out = carry
        block, halo, coeff, cotangent = inputs
        values = block.astype(jnp.float32)
        moved = (values + coeff * (neighbour_sum(values, halo.astype(jnp.float32)) - 4.0 * values)).astype(jnp.bfloat16)
        remapped = band_remap(moved.reshape(4, LEVELS, SIDE * SIDE), remap_weight, remap_band)
        flat = remapped.reshape(FEATURES, SIDE * SIDE)
        pre = jnp.dot(w_in, flat, preferred_element_type=jnp.float32)
        sigma = jax.nn.sigmoid(pre)
        hidden = (pre * sigma).astype(jnp.bfloat16)
        output = (flat.astype(jnp.float32) + jnp.dot(w_out, hidden, preferred_element_type=jnp.float32)).astype(jnp.bfloat16)
        grads = cotangent.reshape(FEATURES, SIDE * SIDE)
        back = jnp.dot(w_out.T, grads, preferred_element_type=jnp.float32)
        slope = (sigma * (1.0 + pre * (1.0 - sigma)) * back).astype(jnp.bfloat16)
        grad_out = grad_out + jnp.dot(grads, hidden.T, preferred_element_type=jnp.float32)
        grad_in = grad_in + jnp.dot(slope, flat.T, preferred_element_type=jnp.float32)
        dflat = grads.astype(jnp.float32) + jnp.dot(w_in.T, slope, preferred_element_type=jnp.float32)
        dmoved = jnp.einsum('kj,fkn->fjn', matrix, dflat.reshape(4, LEVELS, SIDE * SIDE), precision=lax.Precision.HIGHEST)
        dmoved = dmoved.astype(jnp.bfloat16).reshape(4, LEVELS, SIDE, SIDE)
        return ((grad_in, grad_out), (output.reshape(4, LEVELS, SIDE, SIDE), dmoved))
    start = (jnp.zeros((UNITS, FEATURES), jnp.float32), jnp.zeros((FEATURES, UNITS), jnp.float32))
    (grad_in, grad_out), (outputs, dmoved_all) = lax.scan(one_tile, start, (blocks, halos, coeffs, cotangents))
    flux_all = (coeffs[:, None, None, :, :] * dmoved_all.astype(jnp.float32)).astype(jnp.bfloat16)
    flux_halos = tile_halos(flux_all, edge_table)

    def adjoint_tile(inputs):
        dmoved, flux, flux_halo = inputs
        wide = flux.astype(jnp.float32)
        return (dmoved.astype(jnp.float32) - 4.0 * wide + neighbour_sum(wide, flux_halo.astype(jnp.float32))).astype(jnp.bfloat16)
    grads_all = lax.map(adjoint_tile, (dmoved_all, flux_all, flux_halos))
    scale = 1.0 / math.sqrt(COLUMNS)
    state_out = outputs.transpose(1, 2, 0, 3, 4).reshape(4, LEVELS, TILES * SIDE, SIDE)
    grad_state = grads_all.transpose(1, 2, 0, 3, 4).reshape(4, LEVELS, TILES * SIDE, SIDE)
    return (state_out, grad_state, grad_in * scale, grad_out * scale)
```

```python
import functools
import math

import jax
import jax.numpy as jnp
from jax import lax
from jax.experimental import pallas as pl
from jax.experimental.pallas import tpu as pltpu
from jax.sharding import PartitionSpec as P

F32 = jnp.float32
BF16 = jnp.bfloat16
MESH = pl.DeviceIdType.MESH


def dot(a, b, dims=((1,), (0,))):
    return lax.dot_general(a, b, (dims, ((), ())), preferred_element_type=F32)


def body(tiles, state, cot, dif, wcol, bcol, wrow, brow, src, turn, w_in, w_out,
         o_state, o_grad, o_gin, o_gout,
         rel, s_a, g_a, m_a, g_x, m_x, o_x, d_x, o_a, d_a, f_a, edge, strip1, strip2, pick,
         xs, hid, slo, w_out_t, w_in_t, maps, gb, gf, r1, s2, r2, s3, r3, ag,
         ga_s, ga_r, ma_s, ma_r, oa_s, oa_r, da_s, da_r, h1_s, h1_r, h2_s, h2_r,
         p1_s, p1_r, p2_s, p2_r, p3_s, p3_r, p4_s, p4_r, p5_s, p5_r):
    t = lax.axis_index("tile")
    lev = lax.axis_index("lev")
    xpos = lev // 2
    core = lev % 2
    chunk = 1024 // tiles
    scale = 1.0 / math.sqrt(tiles * 4096)

    barrier = pltpu.get_barrier_semaphore()
    for d in range(1, 4):
        pl.semaphore_signal(barrier, inc=1, device_id={"lev": (lev + d) % 4}, device_id_type=MESH)

    def greet(d, _):
        pl.semaphore_signal(barrier, inc=1, device_id={"tile": (t + d) % tiles}, device_id_type=MESH)
        return 0

    lax.fori_loop(1, tiles, greet, 0)

    def rcopy(s, d, ss, rs, i, dev):
        return pltpu.make_async_remote_copy(
            src_ref=s, dst_ref=d, send_sem=ss.at[i], recv_sem=rs.at[i], device_id=dev, device_id_type=MESH)

    def to_columns(a, x, ss, rs, d):
        peer = (lev + d) % 4
        return rcopy(a.at[pl.ds(peer * 8, 8)], x.at[:, :, lev], ss, rs, d - 1, {"lev": peer})

    def to_levels(x, a, ss, rs, d):
        peer = (lev + d) % 4
        return rcopy(x.at[:, :, peer], a.at[pl.ds(lev * 8, 8)], ss, rs, d - 1, {"lev": peer})

    def share(buf, ss, rs, d):
        return rcopy(buf.at[t], buf.at[t], ss, rs, d - 1, {"tile": (t + d) % tiles})

    def each_tile(make, act):
        def step(d, _):
            act(make(d))
            return 0

        lax.fori_loop(1, tiles, step, 0)

    def pack(ref, blocks):
        def step(i, _):
            v = ref[i].astype(F32)
            rel[pl.ds(pl.multiple_of(i * 32, 32), 32), :] = jnp.concatenate([v[:32], v[32:]], axis=1)
            return 0

        lax.fori_loop(0, 64, step, 0, unroll=8)
        for b in range(32):
            blocks[b] = rel[pl.ds(b, 64, stride=32), :].astype(BF16).reshape(4, 16, 128)

    def unpack(ref):
        def step(i, _):
            v = rel[pl.ds(pl.multiple_of(i * 32, 32), 32), :]
            ref[i] = jnp.concatenate([v[:, :64], v[:, 64:]], axis=0).astype(BF16)
            return 0

        lax.fori_loop(0, 64, step, 0, unroll=8)

    row = lax.broadcasted_iota(jnp.int32, (256, 128), 0)
    lane = lax.broadcasted_iota(jnp.int32, (256, 128), 1)
    e = row // 64
    p = row % 64
    side_cell = (p % 32) * 128 + (p // 32) * 64
    cell = jnp.where(e == 0, p, jnp.where(e == 1, 31 * 128 + 64 + p, jnp.where(e == 2, side_cell, side_cell + 63)))
    cell = cell - lane
    pack(state, s_a)
    for b in range(32):
        edge[b] = (cell == b * 128).astype(F32).astype(BF16)

    def find_strips(blocks, strips):
        def step(b, total):
            return total + dot(blocks[b].reshape(64, 128), edge[b], ((1,), (1,)))

        total = lax.fori_loop(0, 32, step, jnp.zeros((64, 256), F32), unroll=4)
        strips[t] = total.astype(BF16)

    find_strips(s_a, strip1)
    pl.semaphore_wait(barrier, tiles + 2)
    each_tile(functools.partial(share, strip1, h1_s, h1_r), lambda c: c.start())

    pack(cot, g_a)
    g_copies = [to_columns(g_a, g_x, ga_s, ga_r, d) for d in range(1, 4)]
    for c in g_copies:
        c.start()
    g_x[:, :, lev] = g_a[pl.ds(lev * 8, 8)]

    row2 = lax.broadcasted_iota(jnp.int32, (256, 256), 0)
    lane2 = lax.broadcasted_iota(jnp.int32, (256, 256), 1)
    wanted = src[...] - row2

    def pick_step(i, _):
        pick[i] = (wanted == i * 256).astype(F32).astype(BF16)
        return 0

    lax.fori_loop(0, tiles, pick_step, 0)
    m = jnp.zeros((256, 256), F32)
    mt = jnp.zeros((256, 256), F32)
    for b in range(4):
        m = m + jnp.where(lane2 == bcol[...] + b, wcol[:, b:b + 1], 0.0)
        mt = mt + jnp.where(row2 == brow[...] + b, wrow[b:b + 1, :], 0.0)
    m_hi = m.astype(BF16)
    mt_hi = mt.astype(BF16)
    maps[0] = m_hi
    maps[1] = (m - m_hi.astype(F32)).astype(BF16)
    maps[2] = mt_hi
    maps[3] = (mt - mt_hi.astype(F32)).astype(BF16)
    w_out_t[...] = w_out[...].T
    w_in_t[...] = w_in[...].T
    dd = jnp.concatenate([dif[:32, :], dif[32:, :]], axis=1)

    def halos(strips):
        def step(i, total):
            return total + dot(strips[i], pick[i])

        h = lax.fori_loop(0, tiles, step, jnp.zeros((64, 256), F32))
        c = turn[0:1, :]
        s = turn[1:2, :]
        u = h[:16]
        v = h[16:32]
        return jnp.concatenate([c * u - s * v, s * u + c * v, h[32:]], axis=0).astype(BF16)

    lane64 = lax.broadcasted_iota(jnp.int32, (64, 128), 1)

    def neighbours(blocks, h, b):
        def at(i):
            return blocks[i].astype(F32).reshape(64, 128)

        v = at(b)
        if b == 0:
            up = jnp.where(lane64 >= 64, pltpu.roll(at(31), 64, 1), 0.0)
        else:
            up = at(b - 1)
        if b == 31:
            down = jnp.where(lane64 < 64, pltpu.roll(at(0), 64, 1), 0.0)
        else:
            down = at(b + 1)
        before = jnp.where(lane64 % 64 == 0, 0.0, pltpu.roll(v, 1, 1))
        after = jnp.where(lane64 % 64 == 63, 0.0, pltpu.roll(v, 127, 1))
        return v, up + down + before + after + dot(h, edge[b])

    each_tile(functools.partial(share, strip1, h1_s, h1_r), lambda c: c.wait())
    h = halos(strip1)
    for b in range(32):
        v, around = neighbours(s_a, h, b)
        moved = v + dd[b:b + 1, :] * (around - 4.0 * v)
        m_a[b] = moved.astype(BF16).reshape(4, 16, 128)
    m_copies = [to_columns(m_a, m_x, ma_s, ma_r, d) for d in range(1, 4)]
    for c in m_copies:
        c.start()
    m_x[:, :, lev] = m_a[pl.ds(lev * 8, 8)]
    for c in g_copies:
        c.wait()
    for c in m_copies:
        c.wait()

    def columns(k, _):
        def pair(ref):
            return jnp.concatenate([ref[2 * k].reshape(256, 128), ref[2 * k + 1].reshape(256, 128)], axis=1)

        at = pl.ds(pl.multiple_of(k * 256, 256), 256)
        moved = pair(m_x)
        g = pair(g_x)
        x = (dot(maps[0], moved) + dot(maps[1], moved)).astype(BF16)
        xs[:, at] = x
        pre = dot(w_in[...], x)
        sigma = jax.nn.sigmoid(pre)
        hidden = (pre * sigma).astype(BF16)
        hid[:, at] = hidden
        slope = (sigma * (1.0 + pre * (1.0 - sigma)) * dot(w_out_t[...], g)).astype(BF16)
        slo[:, at] = slope
        out = (x.astype(F32) + dot(w_out[...], hidden)).astype(BF16)
        dx = g.astype(F32) + dot(w_in_t[...], slope)
        dx_hi = dx.astype(BF16)
        dx_lo = (dx - dx_hi.astype(F32)).astype(BF16)
        dm = (dot(maps[2], dx_hi) + dot(maps[2], dx_lo) + dot(maps[3], dx_hi)).astype(BF16)
        for half in range(2):
            cut = slice(half * 128, half * 128 + 128)
            o_x[2 * k + half] = out[:, cut].reshape(4, 4, 16, 128)
            d_x[2 * k + half] = dm[:, cut].reshape(4, 4, 16, 128)
        return 0

    lax.fori_loop(0, 4, columns, 0)
    d_copies = [to_levels(d_x, d_a, da_s, da_r, d) for d in range(1, 4)]
    for c in d_copies:
        c.start()
    d_a[pl.ds(lev * 8, 8)] = d_x[:, :, lev]

    g_all = jnp.concatenate([g_x[b].reshape(256, 128) for b in range(8)], axis=1)
    for q in range(4):
        gin = dot(slo[q * 256:(q + 1) * 256, :], xs[...], ((1,), (1,)))
        for i in range(2):
            part = gin[:, i * 128:(i + 1) * 128]
            gf[q, i * 256:(i + 1) * 256] = part
            gb[q, i * 256:(i + 1) * 256] = part.astype(BF16)
    for i in range(4):
        gout = dot(g_all, hid[i * 256:(i + 1) * 256, :], ((1,), (1,)))
        for q in range(4):
            for j in range(2):
                part = gout[q * 64:(q + 1) * 64, j * 128:(j + 1) * 128]
                base = 512 + (2 * i + j) * 64
                gf[q, base:base + 64] = part
                gb[q, base:base + 64] = part.astype(BF16)
    mate = {"lev": xpos * 2 + 1 - core}
    across = {"lev": (1 - xpos) * 2 + core}
    first = [rcopy(gb.at[2 * i + 1 - core], r1.at[i], p1_s, p1_r, i, mate) for i in range(2)]

    for c in d_copies:
        c.wait()
    for c in first:
        c.start()
    for b in range(32):
        f_a[b] = (dd[b:b + 1, :] * d_a[b].astype(F32).reshape(64, 128)).astype(BF16).reshape(4, 16, 128)
    find_strips(f_a, strip2)
    each_tile(functools.partial(share, strip2, h2_s, h2_r), lambda c: c.start())

    for c in first:
        c.wait()
    s2[...] = (gf[2 * (1 - xpos) + core] + r1[1 - xpos].astype(F32)).astype(BF16)
    second = rcopy(s2, r2, p2_s, p2_r, 0, across)
    second.start()
    o_copies = [to_levels(o_x, o_a, oa_s, oa_r, d) for d in range(1, 4)]
    for c in o_copies:
        c.start()
    o_a[pl.ds(lev * 8, 8)] = o_x[:, :, lev]

    second.wait()
    s3[...] = (gf[lev] + r1[xpos].astype(F32) + r2[...].astype(F32)).astype(BF16).reshape(tiles, chunk, 128)

    def spread(d):
        other = (t + d) % tiles
        return rcopy(s3.at[other], r3.at[t], p3_s, p3_r, d - 1, {"tile": other})

    each_tile(spread, lambda c: c.start())
    r3[t] = s3[t]

    each_tile(functools.partial(share, strip2, h2_s, h2_r), lambda c: c.wait())
    h = halos(strip2)
    for b in range(32):
        v, around = neighbours(f_a, h, b)
        dm = d_a[b].astype(F32).reshape(64, 128)
        rel[pl.ds(b, 64, stride=32), :] = dm - 4.0 * v + around
    each_tile(spread, lambda c: c.wait())

    def add(i, total):
        return total + r3[i].astype(F32)

    ag[lev, t] = lax.fori_loop(0, tiles, add, jnp.zeros((chunk, 128), F32)).astype(BF16)

    def collect(d):
        return rcopy(ag.at[lev, t], ag.at[lev, t], p4_s, p4_r, d - 1, {"tile": (t + d) % tiles})

    each_tile(collect, lambda c: c.start())
    unpack(o_grad)
    each_tile(collect, lambda c: c.wait())
    last_x = rcopy(ag.at[lev], ag.at[lev], p5_s, p5_r, 0, across)
    last_c = rcopy(ag.at[lev], ag.at[lev], p5_s, p5_r, 1, mate)
    last_x.start()
    last_c.start()
    for c in o_copies:
        c.wait()
    for b in range(32):
        rel[pl.ds(b, 64, stride=32), :] = o_a[b].astype(F32).reshape(64, 128)
    unpack(o_state)
    last_x.wait()
    far = (1 - xpos) * 2 + core
    relay = rcopy(ag.at[far], ag.at[far], p5_s, p5_r, 2, mate)
    relay.start()
    last_c.wait()
    relay.wait()
    for q in range(4):
        whole = ag[q].reshape(1024, 128).astype(F32) * scale
        for i in range(2):
            o_gin[q * 256:(q + 1) * 256, i * 128:(i + 1) * 128] = whole[i * 256:(i + 1) * 256]
        for i in range(8):
            o_gout[q * 64:(q + 1) * 64, i * 128:(i + 1) * 128] = whole[512 + i * 64:576 + i * 64]


def shards(state, state_cotangent, diffusion, remap_weight, remap_band, edge_table, w_in, w_out):
    tiles = lax.axis_size("tile")
    table = edge_table[0]
    place = jnp.arange(64, dtype=jnp.int32)[None, :]
    along = jnp.where(table[:, 2:3] == 1, 63 - place, place)
    src = (table[:, 0:1] * 256 + table[:, 1:2] * 64 + along).reshape(1, 256)
    quarter = jnp.broadcast_to(table[:, 3:4], (4, 64)).reshape(1, 256)
    cosine = (quarter == 0).astype(F32) - (quarter == 2).astype(F32)
    sine = (quarter == 1).astype(F32) - (quarter == 3).astype(F32)
    turn = jnp.concatenate([cosine, sine], axis=0)
    field = jnp.arange(4, dtype=jnp.int32)[:, None] * 64
    band = (field + remap_band[None, :]).reshape(256)
    weight = jnp.tile(remap_weight, (4, 1))
    vm = pltpu.VMEM
    dma = pltpu.SemaphoreType.DMA
    block = vm((32, 4, 16, 128), BF16)
    cols = vm((8, 4, 4, 16, 128), BF16)
    chunk = 1024 // tiles
    out = pl.pallas_call(
        functools.partial(body, tiles),
        out_shape=(
            jax.ShapeDtypeStruct((64, 64, 64), BF16),
            jax.ShapeDtypeStruct((64, 64, 64), BF16),
            jax.ShapeDtypeStruct((1024, 256), F32),
            jax.ShapeDtypeStruct((256, 1024), F32),
        ),
        in_specs=[pl.BlockSpec(memory_space=vm)] * 11,
        out_specs=[pl.BlockSpec(memory_space=vm)] * 4,
        scratch_shapes=[
            vm((2048, 128), F32), block, block, block, cols, cols, cols, cols, block, block, block,
            vm((32, 256, 128), BF16), vm((tiles, 64, 256), BF16), vm((tiles, 64, 256), BF16),
            vm((tiles, 256, 256), BF16),
            vm((256, 1024), BF16), vm((1024, 1024), BF16), vm((1024, 1024), BF16),
            vm((1024, 256), BF16), vm((256, 1024), BF16), vm((4, 256, 256), BF16),
            vm((4, 1024, 128), BF16), vm((4, 1024, 128), F32), vm((2, 1024, 128), BF16),
            vm((1024, 128), BF16), vm((1024, 128), BF16), vm((tiles, chunk, 128), BF16),
            vm((tiles, chunk, 128), BF16), vm((4, tiles, chunk, 128), BF16),
            dma((3,)), dma((3,)), dma((3,)), dma((3,)), dma((3,)), dma((3,)), dma((3,)), dma((3,)),
            dma((tiles - 1,)), dma((tiles - 1,)), dma((tiles - 1,)), dma((tiles - 1,)),
            dma((2,)), dma((2,)), dma((1,)), dma((1,)),
            dma((tiles - 1,)), dma((tiles - 1,)), dma((tiles - 1,)), dma((tiles - 1,)),
            dma((3,)), dma((3,)),
        ],
        compiler_params=pltpu.CompilerParams(
            collective_id=0, has_side_effects=True, vmem_limit_bytes=60 * 1024 * 1024),
    )(
        state.reshape(64, 64, 64), state_cotangent.reshape(64, 64, 64), diffusion,
        weight, band[:, None], weight.T, band[None, :], src, turn, w_in, w_out,
    )
    shape = state.shape
    return out[0].reshape(shape), out[1].reshape(shape), out[2], out[3]


def solution(mesh):
    placed = (
        P(None, "lev", "tile", None),
        P(None, "lev", "tile", None),
        P("tile", None),
        P(),
        P(),
        P("tile", None, None),
        P(),
        P(),
    )
    return jax.shard_map(
        shards,
        mesh=mesh,
        in_specs=placed,
        out_specs=(P(None, "lev", "tile", None), P(None, "lev", "tile", None), P(), P()),
        check_vma=False,
    )
```

```python
import functools
import math

import jax
import jax.numpy as jnp
from jax import lax
from jax.experimental import pallas as pl
from jax.experimental.pallas import tpu as pltpu
from jax.sharding import PartitionSpec as P

F32 = jnp.float32
BF16 = jnp.bfloat16
MESH = pl.DeviceIdType.MESH


def dot(a, b, dims=((1,), (0,))):
    return lax.dot_general(a, b, (dims, ((), ())), preferred_element_type=F32)


def body(tiles, table, state, cot, dif, weight, band, w_in, w_out,
         o_state, o_grad, o_gin, o_gout,
         rel, s_a, g_a, m_a, g_x, m_x, o_x, d_x, o_a, d_a, f_a, edge, strip1, strip2, pick,
         xs, hid, slo, w_out_t, w_in_t, maps,
         gb_in, gf_in, gb_out, gf_out, r1_in, r1_out, s2, r2, s3_in, r3_in, s3_out, r3_out, x_own, x_got, ag_in, ag_out,
         ga_s, ga_r, ma_s, ma_r, oa_s, oa_r, da_s, da_r, h1_s, h1_r, h2_s, h2_r,
         p1_s, p1_r, p2_s, p2_r, p3_s, p3_r, p4_s, p4_r, p5_s, p5_r, p6_s, p6_r, p7_s, p7_r):
    t = lax.axis_index("tile")
    lev = lax.axis_index("lev")
    xpos = lev // 2
    core = lev % 2
    scale = 1.0 / math.sqrt(tiles * 4096)

    barrier = pltpu.get_barrier_semaphore()
    for d in range(1, 4):
        pl.semaphore_signal(barrier, inc=1, device_id={"lev": (lev + d) % 4}, device_id_type=MESH)

    def greet(d, _):
        pl.semaphore_signal(barrier, inc=1, device_id={"tile": (t + d) % tiles}, device_id_type=MESH)
        return 0

    lax.fori_loop(1, tiles, greet, 0)

    def rcopy(s, d, ss, rs, i, dev):
        return pltpu.make_async_remote_copy(
            src_ref=s, dst_ref=d, send_sem=ss.at[i], recv_sem=rs.at[i], device_id=dev, device_id_type=MESH)

    def to_columns(a, x, ss, rs, k, d):
        peer = (lev + d) % 4
        return rcopy(a.at[pl.ds(peer * 8 + 2 * k, 2)], x.at[pl.ds(2 * k, 2), :, lev], ss, rs, k * 3 + d - 1, {"lev": peer})

    def to_levels(x, a, ss, rs, k, d):
        peer = (lev + d) % 4
        return rcopy(x.at[pl.ds(2 * k, 2), :, peer], a.at[pl.ds(lev * 8 + 2 * k, 2)], ss, rs, k * 3 + d - 1, {"lev": peer})

    def share(buf, ss, rs, d):
        return rcopy(buf.at[t], buf.at[t], ss, rs, d - 1, {"tile": (t + d) % tiles})

    def each_tile(make, act):
        def step(d, _):
            act(make(d))
            return 0

        lax.fori_loop(1, tiles, step, 0)

    def pack(ref, blocks):
        def step(i, _):
            v = ref[i].astype(F32)
            rel[pl.ds(pl.multiple_of(i * 32, 32), 32), :] = jnp.concatenate([v[:32], v[32:]], axis=1)
            return 0

        lax.fori_loop(0, 64, step, 0, unroll=8)
        for b in range(32):
            blocks[b] = rel[pl.ds(b, 64, stride=32), :].astype(BF16).reshape(4, 16, 128)

    def unpack(ref):
        def step(i, _):
            v = rel[pl.ds(pl.multiple_of(i * 32, 32), 32), :]
            ref[i] = jnp.concatenate([v[:, :64], v[:, 64:]], axis=0).astype(BF16)
            return 0

        lax.fori_loop(0, 64, step, 0, unroll=8)

    row = lax.broadcasted_iota(jnp.int32, (256, 128), 0)
    lane = lax.broadcasted_iota(jnp.int32, (256, 128), 1)
    e = row // 64
    p = row % 64
    side_cell = (p % 32) * 128 + (p // 32) * 64
    cell = jnp.where(e == 0, p, jnp.where(e == 1, 31 * 128 + 64 + p, jnp.where(e == 2, side_cell, side_cell + 63)))
    cell = cell - lane
    pack(state, s_a)
    for b in range(32):
        edge[b] = (cell == b * 128).astype(F32).astype(BF16)

    def find_strips(blocks, strips):
        def step(b, total):
            return total + dot(blocks[b].reshape(64, 128), edge[b], ((1,), (1,)))

        total = lax.fori_loop(0, 32, step, jnp.zeros((64, 256), F32), unroll=4)
        strips[t] = total.astype(BF16)

    find_strips(s_a, strip1)
    pl.semaphore_wait(barrier, tiles + 2)
    each_tile(functools.partial(share, strip1, h1_s, h1_r), lambda c: c.start())

    pack(cot, g_a)
    g_copies = [to_columns(g_a, g_x, ga_s, ga_r, k, d) for k in range(4) for d in range(1, 4)]
    for c in g_copies:
        c.start()
    g_x[:, :, lev] = g_a[pl.ds(lev * 8, 8)]

    row2 = lax.broadcasted_iota(jnp.int32, (256, 256), 0)
    lane1 = lax.broadcasted_iota(jnp.int32, (1, 256), 1)
    place = lane1 % 64
    src = jnp.zeros((1, 256), jnp.int32)
    quarter = jnp.zeros((1, 256), jnp.int32)
    for i in range(4):
        found = table[0, i, 0] * 256 + table[0, i, 1] * 64 + place + table[0, i, 2] * (63 - 2 * place)
        src = jnp.where(lane1 // 64 == i, found, src)
        quarter = jnp.where(lane1 // 64 == i, jnp.zeros((1, 256), jnp.int32) + table[0, i, 3], quarter)
    cosine = (quarter == 0).astype(F32) - (quarter == 2).astype(F32)
    sine = (quarter == 1).astype(F32) - (quarter == 3).astype(F32)
    wanted = src - row2

    def pick_step(i, _):
        pick[i] = (wanted == i * 256).astype(F32).astype(BF16)
        return 0

    lax.fori_loop(0, tiles, pick_step, 0)
    bands = jnp.concatenate([band[...] + 64 * i for i in range(4)], axis=1)
    weights = jnp.concatenate([weight[...]] * 4, axis=1)
    mt = jnp.zeros((256, 256), F32)
    for b in range(4):
        mt = mt + jnp.where(row2 == bands + b, weights[b:b + 1, :], 0.0)
    m = mt.T
    m_hi = m.astype(BF16)
    mt_hi = mt.astype(BF16)
    maps[0] = m_hi
    maps[1] = (m - m_hi.astype(F32)).astype(BF16)
    maps[2] = mt_hi
    maps[3] = (mt - mt_hi.astype(F32)).astype(BF16)
    w_out_t[...] = w_out[...].T
    w_in_t[...] = w_in[...].T
    dd = jnp.concatenate([dif[:32, :], dif[32:, :]], axis=1)

    def halos(strips):
        def step(i, total):
            return total + dot(strips[i], pick[i])

        h = lax.fori_loop(0, tiles, step, jnp.zeros((64, 256), F32))
        c, s = cosine, sine
        u = h[:16]
        v = h[16:32]
        return jnp.concatenate([c * u - s * v, s * u + c * v, h[32:]], axis=0).astype(BF16)

    lane64 = lax.broadcasted_iota(jnp.int32, (64, 128), 1)

    def neighbours(blocks, h, b):
        def at(i):
            return blocks[i].astype(F32).reshape(64, 128)

        v = at(b)
        if b == 0:
            up = jnp.where(lane64 >= 64, pltpu.roll(at(31), 64, 1), 0.0)
        else:
            up = at(b - 1)
        if b == 31:
            down = jnp.where(lane64 < 64, pltpu.roll(at(0), 64, 1), 0.0)
        else:
            down = at(b + 1)
        before = jnp.where(lane64 % 64 == 0, 0.0, pltpu.roll(v, 1, 1))
        after = jnp.where(lane64 % 64 == 63, 0.0, pltpu.roll(v, 127, 1))
        return v, up + down + before + after + dot(h, edge[b])

    each_tile(functools.partial(share, strip1, h1_s, h1_r), lambda c: c.wait())
    h = halos(strip1)
    m_copies = []
    for k in range(4):
        for b in [8 * j + 2 * k + i for j in range(4) for i in range(2)]:
            v, around = neighbours(s_a, h, b)
            moved = v + dd[b:b + 1, :] * (around - 4.0 * v)
            m_a[b] = moved.astype(BF16).reshape(4, 16, 128)
        m_copies.append([to_columns(m_a, m_x, ma_s, ma_r, k, d) for d in range(1, 4)])
        for c in m_copies[k]:
            c.start()
    m_x[:, :, lev] = m_a[pl.ds(lev * 8, 8)]
    for c in g_copies:
        c.wait()

    def columns(k):
        def pair(ref):
            return jnp.concatenate([ref[2 * k].reshape(256, 128), ref[2 * k + 1].reshape(256, 128)], axis=1)

        at = slice(k * 256, k * 256 + 256)
        moved = pair(m_x)
        g = pair(g_x)
        x = (dot(maps[0], moved) + dot(maps[1], moved)).astype(BF16)
        xs[:, at] = x
        pre = dot(w_in[...], x)
        sigma = jax.nn.sigmoid(pre)
        hidden = (pre * sigma).astype(BF16)
        hid[:, at] = hidden
        slope = (sigma * (1.0 + pre * (1.0 - sigma)) * dot(w_out_t[...], g)).astype(BF16)
        slo[:, at] = slope
        out = (x.astype(F32) + dot(w_out[...], hidden)).astype(BF16)
        dx = g.astype(F32) + dot(w_in_t[...], slope)
        dx_hi = dx.astype(BF16)
        dx_lo = (dx - dx_hi.astype(F32)).astype(BF16)
        dm = (dot(maps[2], dx_hi) + dot(maps[2], dx_lo) + dot(maps[3], dx_hi)).astype(BF16)
        for half in range(2):
            cut = slice(half * 128, half * 128 + 128)
            o_x[2 * k + half] = out[:, cut].reshape(4, 4, 16, 128)
            d_x[2 * k + half] = dm[:, cut].reshape(4, 4, 16, 128)

    d_copies = []
    for k in range(4):
        for c in m_copies[k]:
            c.wait()
        columns(k)
        now = [to_levels(d_x, d_a, da_s, da_r, k, d) for d in range(1, 4)]
        for c in now:
            c.start()
        d_copies += now
    o_copies = [to_levels(o_x, o_a, oa_s, oa_r, k, d) for k in range(4) for d in range(1, 4)]
    for c in o_copies:
        c.start()

    mate = {"lev": xpos * 2 + 1 - core}
    across = {"lev": (1 - xpos) * 2 + core}
    g_all = jnp.concatenate([g_x[b].reshape(256, 128) for b in range(8)], axis=1)
    for i in range(4):
        gout = dot(g_all, hid[i * 256:(i + 1) * 256, :], ((1,), (1,)))
        for q in range(4):
            for j in range(2):
                part = gout[q * 64:(q + 1) * 64, j * 128:(j + 1) * 128]
                base = (2 * i + j) * 64
                gf_out[q, base:base + 64] = part
                gb_out[q, base:base + 64] = part.astype(BF16)
    first_out = [rcopy(gb_out.at[2 * i + 1 - core], r1_out.at[i], p1_s, p1_r, i, mate) for i in range(2)]
    for c in first_out:
        c.start()
    for q in range(4):
        gin = dot(slo[q * 256:(q + 1) * 256, :], xs[...], ((1,), (1,)))
        for i in range(2):
            part = gin[:, i * 128:(i + 1) * 128]
            gf_in[q, i * 256:(i + 1) * 256] = part
            gb_in[q, i * 256:(i + 1) * 256] = part.astype(BF16)
    first_in = [rcopy(gb_in.at[2 * i + 1 - core], r1_in.at[i], p1_s, p1_r, 2 + i, mate) for i in range(2)]
    for c in first_in:
        c.start()
    d_a[pl.ds(lev * 8, 8)] = d_x[:, :, lev]
    o_a[pl.ds(lev * 8, 8)] = o_x[:, :, lev]

    def spread(s3, r3, ss, rs, d):
        other = (t + d) % tiles
        return rcopy(s3.at[other], r3.at[t], ss, rs, d - 1, {"tile": other})

    def collect(ag, part, ss, rs, d):
        return rcopy(ag.at[part, t], ag.at[part, t], ss, rs, d - 1, {"tile": (t + d) % tiles})

    def added(r3):
        def add(i, total):
            return total + r3[i].astype(F32)

        return lax.fori_loop(0, tiles, add, jnp.zeros(r3.shape[1:], F32)).astype(BF16)

    for c in first_out:
        c.wait()
    both = jnp.concatenate([gf_out[2 * i + core] + r1_out[i].astype(F32) for i in range(2)], axis=0)
    s3_out[...] = both.astype(BF16).reshape(s3_out.shape)
    spread_out = functools.partial(spread, s3_out, r3_out, p3_s, p3_r)
    each_tile(spread_out, lambda c: c.start())
    r3_out[t] = s3_out[t]
    for c in first_in:
        c.wait()
    s2[...] = (gf_in[2 * (1 - xpos) + core] + r1_in[1 - xpos].astype(F32)).astype(BF16)
    second = rcopy(s2, r2, p2_s, p2_r, 0, across)
    second.start()

    for c in d_copies:
        c.wait()
    for b in range(32):
        f_a[b] = (dd[b:b + 1, :] * d_a[b].astype(F32).reshape(64, 128)).astype(BF16).reshape(4, 16, 128)
    find_strips(f_a, strip2)
    each_tile(functools.partial(share, strip2, h2_s, h2_r), lambda c: c.start())

    second.wait()
    s3_in[...] = (gf_in[lev] + r1_in[xpos].astype(F32) + r2[...].astype(F32)).astype(BF16).reshape(s3_in.shape)
    spread_in = functools.partial(spread, s3_in, r3_in, p6_s, p6_r)
    each_tile(spread_in, lambda c: c.start())
    r3_in[t] = s3_in[t]

    each_tile(spread_out, lambda c: c.wait())
    x_own[...] = added(r3_out)
    swap = rcopy(x_own, x_got, p2_s, p2_r, 1, across)
    swap.start()

    each_tile(functools.partial(share, strip2, h2_s, h2_r), lambda c: c.wait())
    h = halos(strip2)
    swap.wait()
    ag_out[core, t] = (x_own[...].astype(F32) + x_got[...].astype(F32)).astype(BF16)
    collect_out = functools.partial(collect, ag_out, core, p4_s, p4_r)
    each_tile(collect_out, lambda c: c.start())
    each_tile(spread_in, lambda c: c.wait())
    ag_in[lev, t] = added(r3_in)
    collect_in = functools.partial(collect, ag_in, lev, p7_s, p7_r)
    each_tile(collect_in, lambda c: c.start())

    for b in range(32):
        v, around = neighbours(f_a, h, b)
        dm = d_a[b].astype(F32).reshape(64, 128)
        rel[pl.ds(b, 64, stride=32), :] = dm - 4.0 * v + around
    unpack(o_grad)
    each_tile(collect_in, lambda c: c.wait())
    last_x = rcopy(ag_in.at[lev], ag_in.at[lev], p5_s, p5_r, 0, across)
    last_c = rcopy(ag_in.at[lev], ag_in.at[lev], p5_s, p5_r, 1, mate)
    last_x.start()
    last_c.start()
    each_tile(collect_out, lambda c: c.wait())
    last_o = rcopy(ag_out.at[core], ag_out.at[core], p5_s, p5_r, 3, mate)
    last_o.start()
    for c in o_copies:
        c.wait()
    for b in range(32):
        rel[pl.ds(b, 64, stride=32), :] = o_a[b].astype(F32).reshape(64, 128)
    unpack(o_state)
    last_x.wait()
    far = (1 - xpos) * 2 + core
    relay = rcopy(ag_in.at[far], ag_in.at[far], p5_s, p5_r, 2, mate)
    relay.start()
    last_o.wait()
    for half in range(2):
        whole = ag_out[half].reshape(1024, 128).astype(F32) * scale
        for k in range(2):
            q = 2 * k + half
            for i in range(8):
                base = k * 512 + i * 64
                o_gout[q * 64:(q + 1) * 64, i * 128:(i + 1) * 128] = whole[base:base + 64]
    last_c.wait()
    relay.wait()
    for q in range(4):
        whole = ag_in[q].reshape(512, 128).astype(F32) * scale
        for i in range(2):
            o_gin[q * 256:(q + 1) * 256, i * 128:(i + 1) * 128] = whole[i * 256:(i + 1) * 256]


def shards(state, state_cotangent, diffusion, remap_weight, remap_band, edge_table, w_in, w_out):
    tiles = lax.axis_size("tile")
    vm = pltpu.VMEM
    dma = pltpu.SemaphoreType.DMA
    block = vm((32, 4, 16, 128), BF16)
    cols = vm((8, 4, 4, 16, 128), BF16)
    some_in = vm((tiles, 512 // tiles, 128), BF16)
    some_out = vm((tiles, 1024 // tiles, 128), BF16)
    out = pl.pallas_call(
        functools.partial(body, tiles),
        out_shape=(
            jax.ShapeDtypeStruct((64, 64, 64), BF16),
            jax.ShapeDtypeStruct((64, 64, 64), BF16),
            jax.ShapeDtypeStruct((1024, 256), F32),
            jax.ShapeDtypeStruct((256, 1024), F32),
        ),
        in_specs=[pl.BlockSpec(memory_space=pltpu.SMEM)] + [pl.BlockSpec(memory_space=vm)] * 7,
        out_specs=[pl.BlockSpec(memory_space=vm)] * 4,
        scratch_shapes=[
            vm((2048, 128), F32), block, block, block, cols, cols, cols, cols, block, block, block,
            vm((32, 256, 128), BF16), vm((tiles, 64, 256), BF16), vm((tiles, 64, 256), BF16),
            vm((tiles, 256, 256), BF16),
            vm((256, 1024), BF16), vm((1024, 1024), BF16), vm((1024, 1024), BF16),
            vm((1024, 256), BF16), vm((256, 1024), BF16), vm((4, 256, 256), BF16),
            vm((4, 512, 128), BF16), vm((4, 512, 128), F32), vm((4, 512, 128), BF16), vm((4, 512, 128), F32),
            vm((2, 512, 128), BF16), vm((2, 512, 128), BF16), vm((512, 128), BF16), vm((512, 128), BF16),
            some_in, some_in, some_out, some_out,
            vm((1024 // tiles, 128), BF16), vm((1024 // tiles, 128), BF16),
            vm((4, tiles, 512 // tiles, 128), BF16), vm((2, tiles, 1024 // tiles, 128), BF16),
            *[dma((12,))] * 8, *[dma((tiles - 1,))] * 4, *[dma((4,))] * 2, *[dma((2,))] * 2,
            *[dma((tiles - 1,))] * 4, *[dma((4,))] * 2, *[dma((tiles - 1,))] * 4,
        ],
        compiler_params=pltpu.CompilerParams(
            collective_id=0, has_side_effects=True, vmem_limit_bytes=60 * 1024 * 1024),
    )(
        edge_table, state.reshape(64, 64, 64), state_cotangent.reshape(64, 64, 64), diffusion,
        remap_weight.T, remap_band[None, :], w_in, w_out,
    )
    shape = state.shape
    return out[0].reshape(shape), out[1].reshape(shape), out[2], out[3]


def solution(mesh):
    placed = (
        P(None, "lev", "tile", None),
        P(None, "lev", "tile", None),
        P("tile", None),
        P(),
        P(),
        P("tile", None, None),
        P(),
        P(),
    )
    return jax.shard_map(
        shards,
        mesh=mesh,
        in_specs=placed,
        out_specs=(P(None, "lev", "tile", None), P(None, "lev", "tile", None), P(), P()),
        check_vma=False,
    )
```

```python
import functools
import math

import jax
import jax.numpy as jnp
from jax import lax
from jax.experimental import pallas as pl
from jax.experimental.pallas import tpu as pltpu
from jax.sharding import PartitionSpec as P

F32 = jnp.float32
BF16 = jnp.bfloat16
MESH = pl.DeviceIdType.MESH


def dot(a, b, dims=((1,), (0,))):
    return lax.dot_general(a, b, (dims, ((), ())), preferred_element_type=F32)


def body(tiles, table, state, cot, dif, weight, band, w_in, w_out,
         o_state, o_grad, o_gin, o_gout,
         rel, s_a, g_a, m_a, g_x, m_x, o_x, d_x, o_a, d_a, f_a, edge, strip1, strip2, pick,
         xs, hid, slo, w_out_t, w_in_t, maps,
         gb_in, gf_in, gb_out, gf_out, r1_in, r1_out, s2, r2, s3_in, r3_in, s3_out, r3_out, x_own, x_got, ag_in, ag_out,
         ga_s, ga_r, ma_s, ma_r, oa_s, oa_r, da_s, da_r, h1_s, h1_r, h2_s, h2_r,
         p1_s, p1_r, p2_s, p2_r, p3_s, p3_r, p4_s, p4_r, p5_s, p5_r, p6_s, p6_r, p7_s, p7_r):
    t = lax.axis_index("tile")
    lev = lax.axis_index("lev")
    xpos = lev // 2
    core = lev % 2
    scale = 1.0 / math.sqrt(tiles * 4096)

    barrier = pltpu.get_barrier_semaphore()
    for d in range(1, 4):
        pl.semaphore_signal(barrier, inc=1, device_id={"lev": (lev + d) % 4}, device_id_type=MESH)

    def greet(d, _):
        pl.semaphore_signal(barrier, inc=1, device_id={"tile": (t + d) % tiles}, device_id_type=MESH)
        return 0

    lax.fori_loop(1, tiles, greet, 0)

    def rcopy(s, d, ss, rs, i, dev):
        return pltpu.make_async_remote_copy(
            src_ref=s, dst_ref=d, send_sem=ss.at[i], recv_sem=rs.at[i], device_id=dev, device_id_type=MESH)

    def to_columns(a, x, ss, rs, k, d):
        peer = (lev + d) % 4
        return rcopy(a.at[pl.ds(peer * 8 + 2 * k, 2)], x.at[pl.ds(2 * k, 2), :, lev], ss, rs, k * 3 + d - 1, {"lev": peer})

    def to_levels(x, a, ss, rs, k, d):
        peer = (lev + d) % 4
        return rcopy(x.at[pl.ds(2 * k, 2), :, peer], a.at[pl.ds(lev * 8 + 2 * k, 2)], ss, rs, k * 3 + d - 1, {"lev": peer})

    def share(buf, ss, rs, d):
        return rcopy(buf.at[t], buf.at[t], ss, rs, d - 1, {"tile": (t + d) % tiles})

    def each_tile(make, act):
        def step(d, _):
            act(make(d))
            return 0

        lax.fori_loop(1, tiles, step, 0)

    def pack(ref, blocks):
        def step(i, _):
            v = ref[i].astype(F32)
            rel[pl.ds(pl.multiple_of(i * 32, 32), 32), :] = jnp.concatenate([v[:32], v[32:]], axis=1)
            return 0

        lax.fori_loop(0, 64, step, 0, unroll=8)
        for b in range(32):
            blocks[b] = rel[pl.ds(b, 64, stride=32), :].astype(BF16).reshape(4, 16, 128)

    def unpack(ref):
        def step(i, _):
            v = rel[pl.ds(pl.multiple_of(i * 32, 32), 32), :]
            ref[i] = jnp.concatenate([v[:, :64], v[:, 64:]], axis=0).astype(BF16)
            return 0

        lax.fori_loop(0, 64, step, 0, unroll=8)

    row = lax.broadcasted_iota(jnp.int32, (256, 128), 0)
    lane = lax.broadcasted_iota(jnp.int32, (256, 128), 1)
    e = row // 64
    p = row % 64
    side_cell = (p % 32) * 128 + (p // 32) * 64
    cell = jnp.where(e == 0, p, jnp.where(e == 1, 31 * 128 + 64 + p, jnp.where(e == 2, side_cell, side_cell + 63)))
    cell = cell - lane
    pack(state, s_a)
    for b in range(32):
        edge[b] = (cell == b * 128).astype(F32).astype(BF16)

    def find_strips(blocks, strips):
        def step(b, total):
            return total + dot(blocks[b].reshape(64, 128), edge[b], ((1,), (1,)))

        total = lax.fori_loop(0, 32, step, jnp.zeros((64, 256), F32), unroll=4)
        strips[t] = total.astype(BF16)

    find_strips(s_a, strip1)
    pl.semaphore_wait(barrier, tiles + 2)
    each_tile(functools.partial(share, strip1, h1_s, h1_r), lambda c: c.start())

    pack(cot, g_a)
    g_copies = [to_columns(g_a, g_x, ga_s, ga_r, k, d) for k in range(4) for d in range(1, 4)]
    for c in g_copies:
        c.start()
    g_x[:, :, lev] = g_a[pl.ds(lev * 8, 8)]

    row2 = lax.broadcasted_iota(jnp.int32, (256, 256), 0)
    lane1 = lax.broadcasted_iota(jnp.int32, (1, 256), 1)
    place = lane1 % 64
    src = jnp.zeros((1, 256), jnp.int32)
    quarter = jnp.zeros((1, 256), jnp.int32)
    for i in range(4):
        found = table[0, i, 0] * 256 + table[0, i, 1] * 64 + place + table[0, i, 2] * (63 - 2 * place)
        src = jnp.where(lane1 // 64 == i, found, src)
        quarter = jnp.where(lane1 // 64 == i, jnp.zeros((1, 256), jnp.int32) + table[0, i, 3], quarter)
    cosine = (quarter == 0).astype(F32) - (quarter == 2).astype(F32)
    sine = (quarter == 1).astype(F32) - (quarter == 3).astype(F32)
    wanted = src - row2

    def pick_step(i, _):
        pick[i] = (wanted == i * 256).astype(F32).astype(BF16)
        return 0

    lax.fori_loop(0, tiles, pick_step, 0)
    bands = jnp.concatenate([band[...] + 64 * i for i in range(4)], axis=1)
    weights = jnp.concatenate([weight[...]] * 4, axis=1)
    mt = jnp.zeros((256, 256), F32)
    for b in range(4):
        mt = mt + jnp.where(row2 == bands + b, weights[b:b + 1, :], 0.0)
    m = mt.T
    m_hi = m.astype(BF16)
    mt_hi = mt.astype(BF16)
    maps[0] = m_hi
    maps[1] = (m - m_hi.astype(F32)).astype(BF16)
    maps[2] = mt_hi
    maps[3] = (mt - mt_hi.astype(F32)).astype(BF16)
    w_out_t[...] = w_out[...].T
    w_in_t[...] = w_in[...].T
    dd = jnp.concatenate([dif[:32, :], dif[32:, :]], axis=1)

    def halos(strips):
        def step(i, total):
            return total + dot(strips[i], pick[i])

        h = lax.fori_loop(0, tiles, step, jnp.zeros((64, 256), F32))
        c, s = cosine, sine
        u = h[:16]
        v = h[16:32]
        return jnp.concatenate([c * u - s * v, s * u + c * v, h[32:]], axis=0).astype(BF16)

    lane64 = lax.broadcasted_iota(jnp.int32, (64, 128), 1)

    def neighbours(blocks, h, b):
        def at(i):
            return blocks[i].astype(F32).reshape(64, 128)

        v = at(b)
        if b == 0:
            up = jnp.where(lane64 >= 64, pltpu.roll(at(31), 64, 1), 0.0)
        else:
            up = at(b - 1)
        if b == 31:
            down = jnp.where(lane64 < 64, pltpu.roll(at(0), 64, 1), 0.0)
        else:
            down = at(b + 1)
        before = jnp.where(lane64 % 64 == 0, 0.0, pltpu.roll(v, 1, 1))
        after = jnp.where(lane64 % 64 == 63, 0.0, pltpu.roll(v, 127, 1))
        return v, up + down + before + after + dot(h, edge[b])

    each_tile(functools.partial(share, strip1, h1_s, h1_r), lambda c: c.wait())
    h = halos(strip1)
    m_copies = []
    for k in range(4):
        for b in [8 * j + 2 * k + i for j in range(4) for i in range(2)]:
            v, around = neighbours(s_a, h, b)
            moved = v + dd[b:b + 1, :] * (around - 4.0 * v)
            m_a[b] = moved.astype(BF16).reshape(4, 16, 128)
        m_copies.append([to_columns(m_a, m_x, ma_s, ma_r, k, d) for d in range(1, 4)])
        for c in m_copies[k]:
            c.start()
    m_x[:, :, lev] = m_a[pl.ds(lev * 8, 8)]
    for c in g_copies:
        c.wait()

    def columns(k):
        def pair(ref):
            return jnp.concatenate([ref[2 * k].reshape(256, 128), ref[2 * k + 1].reshape(256, 128)], axis=1)

        at = slice(k * 256, k * 256 + 256)
        moved = pair(m_x)
        g = pair(g_x)
        x = (dot(maps[0], moved) + dot(maps[1], moved)).astype(BF16)
        xs[:, at] = x
        pre = dot(w_in[...], x)
        sigma = jax.nn.sigmoid(pre)
        hidden = (pre * sigma).astype(BF16)
        hid[:, at] = hidden
        slope = (sigma * (1.0 + pre * (1.0 - sigma)) * dot(w_out_t[...], g)).astype(BF16)
        slo[:, at] = slope
        out = (x.astype(F32) + dot(w_out[...], hidden)).astype(BF16)
        dx = g.astype(F32) + dot(w_in_t[...], slope)
        dx_hi = dx.astype(BF16)
        dx_lo = (dx - dx_hi.astype(F32)).astype(BF16)
        dm = (dot(maps[2], dx_hi) + dot(maps[2], dx_lo) + dot(maps[3], dx_hi)).astype(BF16)
        for half in range(2):
            cut = slice(half * 128, half * 128 + 128)
            o_x[2 * k + half] = out[:, cut].reshape(4, 4, 16, 128)
            d_x[2 * k + half] = dm[:, cut].reshape(4, 4, 16, 128)

    d_copies = []
    for k in range(4):
        for c in m_copies[k]:
            c.wait()
        columns(k)
        now = [to_levels(d_x, d_a, da_s, da_r, k, d) for d in range(1, 4)]
        for c in now:
            c.start()
        d_copies += now

    mate = {"lev": xpos * 2 + 1 - core}
    across = {"lev": (1 - xpos) * 2 + core}
    g_all = jnp.concatenate([g_x[b].reshape(256, 128) for b in range(8)], axis=1)
    for i in range(4):
        gout = dot(g_all, hid[i * 256:(i + 1) * 256, :], ((1,), (1,)))
        for q in range(4):
            for j in range(2):
                part = gout[q * 64:(q + 1) * 64, j * 128:(j + 1) * 128]
                base = (2 * i + j) * 64
                gf_out[q, base:base + 64] = part
                gb_out[q, base:base + 64] = part.astype(BF16)
    first_out = [rcopy(gb_out.at[2 * i + 1 - core], r1_out.at[i], p1_s, p1_r, i, mate) for i in range(2)]
    for c in first_out:
        c.start()
    for q in range(4):
        gin = dot(slo[q * 256:(q + 1) * 256, :], xs[...], ((1,), (1,)))
        for i in range(2):
            part = gin[:, i * 128:(i + 1) * 128]
            gf_in[q, i * 256:(i + 1) * 256] = part
            gb_in[q, i * 256:(i + 1) * 256] = part.astype(BF16)
    first_in = [rcopy(gb_in.at[2 * i + 1 - core], r1_in.at[i], p1_s, p1_r, 2 + i, mate) for i in range(2)]
    for c in first_in:
        c.start()
    d_a[pl.ds(lev * 8, 8)] = d_x[:, :, lev]
    o_a[pl.ds(lev * 8, 8)] = o_x[:, :, lev]

    def spread(s3, r3, ss, rs, d):
        other = (t + d) % tiles
        return rcopy(s3.at[other], r3.at[t], ss, rs, d - 1, {"tile": other})

    def collect(ag, part, ss, rs, d):
        return rcopy(ag.at[part, t], ag.at[part, t], ss, rs, d - 1, {"tile": (t + d) % tiles})

    def added(r3):
        def add(i, total):
            return total + r3[i].astype(F32)

        return lax.fori_loop(0, tiles, add, jnp.zeros(r3.shape[1:], F32)).astype(BF16)

    for c in first_out:
        c.wait()
    both = jnp.concatenate([gf_out[2 * i + core] + r1_out[i].astype(F32) for i in range(2)], axis=0)
    s3_out[...] = both.astype(BF16).reshape(s3_out.shape)
    spread_out = functools.partial(spread, s3_out, r3_out, p3_s, p3_r)
    each_tile(spread_out, lambda c: c.start())
    r3_out[t] = s3_out[t]
    for c in first_in:
        c.wait()
    s2[...] = (gf_in[2 * (1 - xpos) + core] + r1_in[1 - xpos].astype(F32)).astype(BF16)
    second = rcopy(s2, r2, p2_s, p2_r, 0, across)
    second.start()
    o_copies = [to_levels(o_x, o_a, oa_s, oa_r, k, d) for k in range(4) for d in range(1, 4)]
    for c in o_copies:
        c.start()

    for c in d_copies:
        c.wait()
    for b in range(32):
        f_a[b] = (dd[b:b + 1, :] * d_a[b].astype(F32).reshape(64, 128)).astype(BF16).reshape(4, 16, 128)
    find_strips(f_a, strip2)
    each_tile(functools.partial(share, strip2, h2_s, h2_r), lambda c: c.start())

    second.wait()
    s3_in[...] = (gf_in[lev] + r1_in[xpos].astype(F32) + r2[...].astype(F32)).astype(BF16).reshape(s3_in.shape)
    spread_in = functools.partial(spread, s3_in, r3_in, p6_s, p6_r)
    each_tile(spread_in, lambda c: c.start())
    r3_in[t] = s3_in[t]

    each_tile(spread_out, lambda c: c.wait())
    x_own[...] = added(r3_out)
    swap = rcopy(x_own, x_got, p2_s, p2_r, 1, across)
    swap.start()

    each_tile(functools.partial(share, strip2, h2_s, h2_r), lambda c: c.wait())
    h = halos(strip2)
    swap.wait()
    ag_out[core, t] = (x_own[...].astype(F32) + x_got[...].astype(F32)).astype(BF16)
    collect_out = functools.partial(collect, ag_out, core, p4_s, p4_r)
    each_tile(collect_out, lambda c: c.start())
    each_tile(spread_in, lambda c: c.wait())
    ag_in[lev, t] = added(r3_in)
    collect_in = functools.partial(collect, ag_in, lev, p7_s, p7_r)
    each_tile(collect_in, lambda c: c.start())

    for b in range(32):
        v, around = neighbours(f_a, h, b)
        dm = d_a[b].astype(F32).reshape(64, 128)
        rel[pl.ds(b, 64, stride=32), :] = dm - 4.0 * v + around
    each_tile(collect_in, lambda c: c.wait())
    last_x = rcopy(ag_in.at[lev], ag_in.at[lev], p5_s, p5_r, 0, across)
    last_c = rcopy(ag_in.at[lev], ag_in.at[lev], p5_s, p5_r, 1, mate)
    last_x.start()
    last_c.start()
    unpack(o_grad)
    each_tile(collect_out, lambda c: c.wait())
    last_o = rcopy(ag_out.at[core], ag_out.at[core], p5_s, p5_r, 3, mate)
    last_o.start()
    for c in o_copies:
        c.wait()
    for b in range(32):
        rel[pl.ds(b, 64, stride=32), :] = o_a[b].astype(F32).reshape(64, 128)
    unpack(o_state)
    last_x.wait()
    far = (1 - xpos) * 2 + core
    relay = rcopy(ag_in.at[far], ag_in.at[far], p5_s, p5_r, 2, mate)
    relay.start()
    last_o.wait()
    for half in range(2):
        whole = ag_out[half].reshape(1024, 128).astype(F32) * scale
        for k in range(2):
            q = 2 * k + half
            for i in range(8):
                base = k * 512 + i * 64
                o_gout[q * 64:(q + 1) * 64, i * 128:(i + 1) * 128] = whole[base:base + 64]
    last_c.wait()
    relay.wait()
    for q in range(4):
        whole = ag_in[q].reshape(512, 128).astype(F32) * scale
        for i in range(2):
            o_gin[q * 256:(q + 1) * 256, i * 128:(i + 1) * 128] = whole[i * 256:(i + 1) * 256]


def shards(state, state_cotangent, diffusion, remap_weight, remap_band, edge_table, w_in, w_out):
    tiles = lax.axis_size("tile")
    vm = pltpu.VMEM
    dma = pltpu.SemaphoreType.DMA
    block = vm((32, 4, 16, 128), BF16)
    cols = vm((8, 4, 4, 16, 128), BF16)
    some_in = vm((tiles, 512 // tiles, 128), BF16)
    some_out = vm((tiles, 1024 // tiles, 128), BF16)
    out = pl.pallas_call(
        functools.partial(body, tiles),
        out_shape=(
            jax.ShapeDtypeStruct((64, 64, 64), BF16),
            jax.ShapeDtypeStruct((64, 64, 64), BF16),
            jax.ShapeDtypeStruct((1024, 256), F32),
            jax.ShapeDtypeStruct((256, 1024), F32),
        ),
        in_specs=[pl.BlockSpec(memory_space=pltpu.SMEM)] + [pl.BlockSpec(memory_space=vm)] * 7,
        out_specs=[pl.BlockSpec(memory_space=vm)] * 4,
        scratch_shapes=[
            vm((2048, 128), F32), block, block, block, cols, cols, cols, cols, block, block, block,
            vm((32, 256, 128), BF16), vm((tiles, 64, 256), BF16), vm((tiles, 64, 256), BF16),
            vm((tiles, 256, 256), BF16),
            vm((256, 1024), BF16), vm((1024, 1024), BF16), vm((1024, 1024), BF16),
            vm((1024, 256), BF16), vm((256, 1024), BF16), vm((4, 256, 256), BF16),
            vm((4, 512, 128), BF16), vm((4, 512, 128), F32), vm((4, 512, 128), BF16), vm((4, 512, 128), F32),
            vm((2, 512, 128), BF16), vm((2, 512, 128), BF16), vm((512, 128), BF16), vm((512, 128), BF16),
            some_in, some_in, some_out, some_out,
            vm((1024 // tiles, 128), BF16), vm((1024 // tiles, 128), BF16),
            vm((4, tiles, 512 // tiles, 128), BF16), vm((2, tiles, 1024 // tiles, 128), BF16),
            *[dma((12,))] * 8, *[dma((tiles - 1,))] * 4, *[dma((4,))] * 2, *[dma((2,))] * 2,
            *[dma((tiles - 1,))] * 4, *[dma((4,))] * 2, *[dma((tiles - 1,))] * 4,
        ],
        compiler_params=pltpu.CompilerParams(
            collective_id=0, has_side_effects=True, vmem_limit_bytes=60 * 1024 * 1024),
    )(
        edge_table, state.reshape(64, 64, 64), state_cotangent.reshape(64, 64, 64), diffusion,
        remap_weight.T, remap_band[None, :], w_in, w_out,
    )
    shape = state.shape
    return out[0].reshape(shape), out[1].reshape(shape), out[2], out[3]


def solution(mesh):
    placed = (
        P(None, "lev", "tile", None),
        P(None, "lev", "tile", None),
        P("tile", None),
        P(),
        P(),
        P("tile", None, None),
        P(),
        P(),
    )
    return jax.shard_map(
        shards,
        mesh=mesh,
        in_specs=placed,
        out_specs=(P(None, "lev", "tile", None), P(None, "lev", "tile", None), P(), P()),
        check_vma=False,
    )
```
